512 devices in a mesh: dp: 64 (over x, z, core), tensor: 8 (over y).
Axes of the slice: x: 4, y: 8, z: 8, core: 2. Of those that a mesh axis runs over, the one named last changes fastest.
Arguments:
- instances: bfloat16 [8192, 1024], P('dp', 'tensor'), may hold values from -6 to 6
- cluster_weights: bfloat16 [128, 256, 1024], P('dp', None, 'tensor'), may hold values from -0.1875 to 0.1875
- cluster_home: int32 [128], replicated, may hold values from 0 to 127, each once
- shortlist: int32 [8192, 20], P('dp'), may hold values from 0 to 127, all different within a row; in each aligned block of 128 rows (0 to 127, 128 to 255, ...) at most 40 rows name the same one
- positives: int32 [8192, 32], P('dp'), may hold values from 0 to 5119
Outputs:
- instance_grad: bfloat16 [8192, 1024], P('dp', 'tensor')
- weight_grad: bfloat16 [128, 256, 1024], P('dp', None, 'tensor')
The draws below stay inside these ranges and needn't reach their ends.
Inputs may be any that keep to these rules, and one draw needn't show every extreme that they name: `shortlist`: each row names 20 different clusters. Within the rows of one index of dp (aligned blocks of 128 rows) no cluster is named by more than 40 rows, a bound that some block reaches. Every cluster is named somewhere. `cluster_home`: each cluster has its own storage row. `positives`: A code may appear more than once in a row.
All inputs are finite; a program needn't handle non-finite values.
Results may differ from the reference program's by a relative error of at most 0.0051.
Values may be sent and summed in bfloat16 or wider, within the bound.
No kernel may reach another device: no remote copies, remote signals or barrier semaphores. Data moves between devices by JAX's collectives and lax.ppermute only.
A program may use at most 64 MiB of HBM per device.

```python
import math
import jax
import jax.numpy as jnp
import numpy as np
from jax import lax

D = 1024
L = 256
K = 20
P_SIZE = 32
B_DEV = 128
INSTANCES = 8192
C = 128
MOST = 40
PAIRS_CL = 1280
N_DP = 64


def place_ends(values, key, least, largest):
    longest = values.shape.index(max(values.shape))
    spots = []
    for shift in (0, 1):
        where = [jax.random.randint(jax.random.fold_in(key, axis), (), 0, length) for axis, length in enumerate(values.shape)]
        where[longest] = (where[longest] + shift) % values.shape[longest]
        spots.append(tuple(where))
    return values.at[spots[0]].set(least).at[spots[1]].set(largest)


def level_of(rng, dims, split, least, top_value):
    level, own = 1.0, jax.random.fold_in(rng, 6)
    for dim, blocks in split:
        steps = jnp.exp(jax.random.uniform(jax.random.fold_in(own, dim), (blocks,), jnp.float32, least / len(split), top_value / len(split)))
        level = level * jnp.repeat(steps, dims[dim] // blocks).reshape([-1 if axis == dim else 1 for axis in range(len(dims))])
    return level


def deal_out(rng, own, number, rows, count, top, bound, slope):
    ranking = jax.random.permutation(rng, count)
    packed, ordinary = portions_of(count, rows * top, bound, slope, True), portions_of(count, rows * top, bound, slope, False)
    places = jnp.arange(count)

    def named(tallies, offset_by):
        used = int((tallies > 0).sum())
        fixed = max(1, used // 4)
        passed = fixed + (places - fixed + offset_by * (used - fixed)) % max(1, count - fixed)
        return jnp.zeros((count,), jnp.int32).at[ranking[jnp.where(places < fixed, places, passed)]].set(jnp.asarray(tallies, jnp.int32))

    tallies = jnp.where(number % 4 == 0, named(packed, number // 4), named(ordinary, number - number // 4 - 1))
    mixed = jax.random.permutation(jax.random.fold_in(own, 3), count)
    giver, receiver = mixed[0:count // 2 * 2:2], mixed[1:count // 2 * 2:2]
    margin = jnp.minimum(tallies[giver] - 1, bound - tallies[receiver]) // 2
    margin = jnp.where((giver == ranking[0]) | (receiver == ranking[0]) | (tallies[receiver] == 0), 0, jnp.maximum(margin, 0))
    passed = jax.random.randint(jax.random.fold_in(own, 4), (count // 2,), 0, 1 << 20) % (margin + 1)
    tallies = tallies.at[giver].add(-passed).at[receiver].add(passed)
    items = jnp.searchsorted(jnp.cumsum(tallies), jnp.arange(rows * top), side="right").astype(jnp.int32)
    grid = items.reshape(top, rows).T
    grid = grid[jax.random.permutation(jax.random.fold_in(own, 1), rows)]
    offset_by = jax.random.randint(jax.random.fold_in(own, 2), (rows, 1), 0, top)
    return jnp.take_along_axis(grid, (jnp.arange(top)[None, :] + offset_by) % top, axis=1)


def portions_of(count, total, bound, lean, full):
    loads = [(1 << 20) // math.isqrt(grade ** lean) + 1 for grade in range(1, count + 1)]
    largest = bound if full else min(bound, max(-(-total // count), total * loads[0] // sum(loads)))
    least = 1 if total - largest >= count - 1 else 0
    given, rest = [largest] + [least] * (count - 1), total - largest - least * (count - 1)
    while rest > 0:
        free = [i for i in range(1, count) if given[i] < largest] or [i for i in range(1, count) if given[i] < bound]
        pool, budget = sum([loads[i] for i in free]), rest
        for i in free:
            addition = min(bound - given[i], max(1, budget * loads[i] // pool), rest)
            given[i] = given[i] + addition
            rest = rest - addition
    return np.array(given)


def noise(rng, extent, scale, limit, split=(), kind=jnp.bfloat16):
    array = jax.random.normal(rng, extent, jnp.float32) * scale
    if len(split) > 0:
        array = level_of(rng, extent, split, -0.22, 0.18) * array
    return jnp.clip(array, min=-limit, max=limit).astype(kind)


def setup_inputs(seed: int = 0) -> dict:
    splits = jax.random.split(jax.random.key(seed), 6)
    instances = noise(splits[0], (INSTANCES, D), 1.0, 6.0, ((0, 64), (1, 8)))
    cluster_weights = noise(splits[1], (C, L, D), D ** -0.5, 0.1875, ((0, 64), (2, 8)))
    cluster_home = jax.random.permutation(splits[2], C).astype(jnp.int32)
    shortlist_keys = jax.random.split(jax.random.fold_in(splits[3], 1), INSTANCES // B_DEV)
    shortlist_turns = jax.random.permutation(jax.random.fold_in(splits[3], 3), INSTANCES // B_DEV)
    shortlist = jax.vmap(lambda own, number: deal_out(jax.random.fold_in(splits[3], 2), own, number, B_DEV, C, K, MOST, 2))(shortlist_keys, shortlist_turns).reshape((INSTANCES, K))
    positives = place_ends(jax.random.randint(splits[4], (INSTANCES, P_SIZE), 0, K * L), jax.random.fold_in(splits[4], 1), 0, (K * L) - 1).astype(jnp.int32)
    return {"instances": instances, "cluster_weights": cluster_weights, "cluster_home": cluster_home, "shortlist": shortlist, "positives": positives}


def reference(instances, cluster_weights, cluster_home, shortlist, positives):
    total_rows, width = instances.shape
    clusters, labels, _ = cluster_weights.shape
    picks = shortlist.shape[1]
    block_rows = total_rows // N_DP
    capacity = N_DP * MOST
    cluster_ids = jnp.arange(clusters, dtype=jnp.int32)
    scale = 1.0 / math.sqrt(PAIRS_CL)

    def block_arrival(block_short):
        chosen = block_short.reshape(-1)
        one_hot = (chosen[:, None] == cluster_ids[None, :]).astype(jnp.int32)
        return lax.optimization_barrier(jnp.sum(one_hot * jnp.cumsum(one_hot, axis=0), axis=1)) - 1
    arrival = lax.map(block_arrival, shortlist.reshape(N_DP, block_rows, picks))
    seat = (jnp.arange(N_DP, dtype=jnp.int32)[:, None] * MOST + arrival).reshape(-1).astype(jnp.int32)
    pair_ids = jnp.arange(total_rows * picks, dtype=jnp.int32)
    table = jnp.full((clusters, capacity), -1, jnp.int32).at[shortlist.reshape(-1), seat].set(pair_ids)
    label_ids = jnp.arange(labels, dtype=jnp.int32)

    def per_cluster(accum, cluster):
        pair_index = table[cluster]
        present = pair_index >= 0
        safe_index = jnp.maximum(pair_index, 0)
        row_index = safe_index // picks
        pick_index = safe_index % picks
        rows = instances[row_index] * present[:, None].astype(jnp.bfloat16)
        weights = cluster_weights[cluster_home[cluster]]
        scores = jnp.dot(rows, weights.T, preferred_element_type=jnp.float32)
        codes = pick_index[:, None] * labels + label_ids[None, :]
        own_pos = positives[row_index]
        hits = jnp.any(own_pos[:, :, None] == codes[:, None, :], axis=1) & present[:, None]
        targets = hits.astype(jnp.float32)
        grad_scores = (jax.nn.sigmoid(scores) - targets).astype(jnp.bfloat16)
        pair_grad = jnp.dot(grad_scores, weights, preferred_element_type=jnp.float32).astype(jnp.bfloat16)
        addend = jnp.where(present[:, None], pair_grad.astype(jnp.float32), jnp.float32(0.0))
        accum = accum.at[row_index].add(addend)
        weight_part = jnp.dot(grad_scores.T, rows, preferred_element_type=jnp.float32) * scale
        return (accum, weight_part)
    start = jnp.zeros((total_rows, width), jnp.float32)
    accum, weight_parts = lax.scan(per_cluster, start, cluster_ids)
    weight_grad = jnp.zeros_like(weight_parts).at[cluster_home].set(weight_parts)
    return (accum.astype(jnp.bfloat16), weight_grad.astype(jnp.bfloat16))
```

```python
import functools
import math

import jax
import jax.numpy as jnp
from jax import lax
from jax.experimental import pallas as pl
from jax.experimental.pallas import tpu as pltpu
from jax.sharding import Mesh, PartitionSpec as P

NX, NZ, NC = 4, 8, 2
LABEL_BITS = 8


def prep_kernel(ids_ref, home_ref, short_ref, pos_ref, out_ref, full_ref):
    short = short_ref[...]
    pos = pos_ref[...]
    picks, rows = short.shape

    def look(c, slots):
        return jnp.where(short == c, home_ref[c], slots)

    slots = lax.fori_loop(0, home_ref.shape[0], look, jnp.zeros_like(short), unroll=8)
    pick = lax.shift_right_logical(pos, LABEL_BITS)
    pos_slot = jnp.zeros_like(pos)
    for k in range(picks):
        pos_slot = jnp.where(pick == k, slots[k : k + 1, :], pos_slot)
    label = pos & ((1 << LABEL_BITS) - 1)
    pad = jnp.full((128 - picks - 2 * pos.shape[0], rows), -1, jnp.int32)
    facts = jnp.concatenate([pos_slot, label, slots, pad], axis=0).astype(jnp.float32)
    full_ref[...] = facts.T.astype(jnp.bfloat16)
    share = out_ref.shape[0]
    out_ref[...] = full_ref[pl.ds(pl.multiple_of(ids_ref[1] * share, share), share), :]


def main_kernel(n_pos, n_picks, first, ids_ref, *refs):
    if first:
        x_ref, w_ref, ig_ref, wg_ref = refs
    else:
        x_ref, w_ref, wg_in_ref, ig_ref, wg_ref = refs
    tiles, feats = x_ref.shape[0], x_ref.shape[1] - 1
    rows = tiles * x_ref.shape[2]
    labels = w_ref.shape[1]
    x = jnp.concatenate([x_ref[:, f].reshape(rows, 128) for f in range(feats)], axis=1)
    w = jnp.concatenate([w_ref[f] for f in range(feats)], axis=1)
    scores = lax.dot_general(w, x, (((1,), (1,)), ((), ())), preferred_element_type=jnp.float32)

    facts = x_ref[:, feats].reshape(rows, 128).astype(jnp.float32).T.astype(jnp.int32)
    base = ids_ref[0] * 2
    pos_slot = facts[:n_pos] - base
    label = facts[n_pos : 2 * n_pos]
    slots = facts[2 * n_pos : 2 * n_pos + 24] - base
    held = (pos_slot == 0) | (pos_slot == 1)
    key = jnp.where(held, pos_slot * (labels // 2) + label, -1)
    word, bit = key >> 5, jnp.left_shift(jnp.int32(1), key & 31)
    lines = lax.broadcasted_iota(jnp.int32, (labels // 32, rows), 0)
    words = jnp.zeros((labels // 32, rows), jnp.int32)
    for p in range(n_pos):
        words = words | jnp.where(word[p : p + 1] == lines, bit[p : p + 1], 0)
    shifts = lax.broadcasted_iota(jnp.int32, (labels // 32, 32, rows), 1)
    bits = lax.shift_right_logical(jnp.broadcast_to(words[:, None, :], shifts.shape), shifts) & 1
    targets = bits.reshape(labels, rows).astype(jnp.float32)
    grad = jax.nn.sigmoid(scores) - targets
    halves = []
    for j in range(2):
        named = jnp.max((slots == j).astype(jnp.float32), axis=0, keepdims=True)
        halves.append(grad[j * (labels // 2) : (j + 1) * (labels // 2)] * named)
    grad = jnp.concatenate(halves, axis=0).astype(jnp.bfloat16)

    ig = lax.dot_general(grad, w, (((0,), (0,)), ((), ())), preferred_element_type=jnp.float32)
    ig = ig.astype(ig_ref.dtype)
    wg = jnp.dot(grad, x, preferred_element_type=jnp.float32)

    @pl.when(pl.program_id(0) == 0)
    def _():
        if first:
            wg_ref[...] = jnp.zeros_like(wg_ref)
        else:
            wg_ref[...] = wg_in_ref[...]

    for f in range(feats):
        ig_ref[:, f] = ig[:, f * 128 : (f + 1) * 128].reshape(tiles, -1, 128)
        wg_ref[f] += wg[:, f * 128 : (f + 1) * 128]


def gradients(ids, x, w, wg, out_type, n_pos, n_picks, steps):
    blocks, width, sub, _ = x.shape
    feats, labels, _ = w.shape
    tiles = blocks // steps
    first = wg is None
    whole = pl.BlockSpec((feats, labels, 128), lambda i, s: (0, 0, 0))
    in_specs = [pl.BlockSpec((tiles, width, sub, 128), lambda i, s: (i, 0, 0, 0)), whole]
    operands = [x, w]
    if not first:
        in_specs.append(whole)
        operands.append(wg)
    flops = 6 * blocks * sub * feats * 128 * labels
    return pl.pallas_call(
        functools.partial(main_kernel, n_pos, n_picks, first),
        out_shape=(
            jax.ShapeDtypeStruct((blocks, feats, sub, 128), out_type),
            jax.ShapeDtypeStruct((feats, labels, 128), jnp.float32),
        ),
        grid_spec=pltpu.PrefetchScalarGridSpec(
            num_scalar_prefetch=1,
            grid=(steps,),
            in_specs=in_specs,
            out_specs=(pl.BlockSpec((tiles, feats, sub, 128), lambda i, s: (i, 0, 0, 0)), whole),
        ),
        compiler_params=pltpu.CompilerParams(vmem_limit_bytes=40 * 1024 * 1024),
        cost_estimate=pl.CostEstimate(flops=flops, bytes_accessed=6 << 20, transcendentals=blocks * sub * labels),
    )(ids, *operands)


def spread(block, axis, size):
    copies = jnp.broadcast_to(block[None], (size, *block.shape))
    return lax.all_to_all(copies, axis, split_axis=0, concat_axis=0, tiled=True)


def collect(parts, axis):
    got = lax.all_to_all(parts.astype(jnp.bfloat16), axis, split_axis=0, concat_axis=0, tiled=True)
    return jnp.sum(got.astype(jnp.float32), axis=0)


def shards(instances, cluster_weights, cluster_home, shortlist, positives):
    ny = lax.axis_size("y")
    rows, part = instances.shape
    owned, labels, _ = cluster_weights.shape
    picks, n_pos = shortlist.shape[1], positives.shape[1]
    clusters = cluster_home.shape[0]
    share = rows // ny
    scale = 1.0 / math.sqrt(rows * picks // owned)
    ids = jnp.stack([lax.axis_index(("x", "z", "c")), lax.axis_index("y")]).astype(jnp.int32)

    w = lax.all_gather(cluster_weights.reshape(owned * labels, part), "y", axis=0)

    facts = pl.pallas_call(
        prep_kernel,
        out_shape=jax.ShapeDtypeStruct((share, 128), jnp.bfloat16),
        in_specs=[pl.BlockSpec(memory_space=pltpu.SMEM)] * 2 + [pl.BlockSpec(memory_space=pltpu.VMEM)] * 2,
        out_specs=pl.BlockSpec(memory_space=pltpu.VMEM),
        scratch_shapes=[pltpu.VMEM((rows, 128), jnp.bfloat16)],
    )(ids, cluster_home, shortlist.T, positives.T)

    own = lax.all_to_all(instances.reshape(ny, share, part), "y", split_axis=0, concat_axis=0, tiled=True)
    own = jnp.concatenate([own, facts[None]], axis=0)
    line = spread(own, "z", NZ)
    mine = spread(line, "x", NX).reshape(NX * NZ, ny + 1, share, 128)
    swap = [(0, 1), (1, 0)]
    theirs = lax.ppermute(mine, "c", swap)

    ig_mine, wg = gradients(ids, mine, w, None, jnp.float32, n_pos, picks, 2)
    ig_theirs, wg = gradients(ids, theirs, w, wg, jnp.bfloat16, n_pos, picks, 2)

    weight_sum = lax.psum_scatter(wg, "y", scatter_dimension=0)
    ig = ig_mine + lax.ppermute(ig_theirs, "c", swap).astype(jnp.float32)
    ig = collect(ig.reshape(NX, NZ, ny, share, 128), "x")
    ig = collect(ig, "z").astype(jnp.bfloat16)
    ig = lax.all_to_all(ig, "y", split_axis=0, concat_axis=0, tiled=True)
    weight_grad = (weight_sum * scale).astype(jnp.bfloat16).reshape(owned, labels, part)
    return ig.reshape(rows, part), weight_grad


def solution(mesh):
    fine = Mesh(mesh.devices.reshape(NX, NZ, NC, -1), ("x", "z", "c", "y"))
    dp = ("x", "z", "c")
    return jax.shard_map(
        shards,
        mesh=fine,
        in_specs=(P(dp, "y"), P(dp, None, "y"), P(), P(dp, None), P(dp, None)),
        out_specs=(P(dp, "y"), P(dp, None, "y")),
        check_vma=False,
    )
```

```python
import functools
import math

import jax
import jax.numpy as jnp
from jax import lax
from jax.experimental import pallas as pl
from jax.experimental.pallas import tpu as pltpu
from jax.sharding import Mesh, PartitionSpec as P

NX, NZ, NC = 4, 8, 2
LABEL_BITS = 8


def prep_kernel(ids_ref, home_ref, short_ref, pos_ref, x_ref, out_ref):
    short = short_ref[...]
    pos = pos_ref[...]
    picks, rows = short.shape

    def look(c, slots):
        return jnp.where(short == c, home_ref[c], slots)

    slots = lax.fori_loop(0, home_ref.shape[0], look, jnp.zeros_like(short), unroll=8)
    pick = lax.shift_right_logical(pos, LABEL_BITS)
    pos_slot = jnp.zeros_like(pos)
    for k in range(picks):
        pos_slot = jnp.where(pick == k, slots[k : k + 1, :], pos_slot)
    label = pos & ((1 << LABEL_BITS) - 1)
    pad = jnp.full((128 - picks - 2 * pos.shape[0], rows), -1, jnp.int32)
    facts = jnp.concatenate([pos_slot, label, slots, pad], axis=0).astype(jnp.float32).T
    copies, parts = out_ref.shape[0], out_ref.shape[1]
    share = rows // parts
    x = x_ref[...].astype(jnp.float32)
    line = lax.broadcasted_iota(jnp.int32, (8, 128), 0)
    for t in range(parts):
        known = []
        for i in range(share // 8):
            tile = facts[t * share + i * 8 : t * share + i * 8 + 8]
            known.append(jnp.sum(jnp.where(line == ids_ref[1], tile, 0.0), axis=0, keepdims=True))
        pairs = [x[t * share + j : t * share + j + 2] for j in range(0, share, 2)]
        message = jnp.concatenate([*pairs, jnp.concatenate(known, axis=0)], axis=1).astype(out_ref.dtype)
        for c in range(copies):
            out_ref[c, t] = message


def repack_kernel(in_ref, out_ref):
    copies, zs, _, share, _ = out_ref.shape
    feats = in_ref.shape[1]
    for z in range(zs):
        known = []
        for f in range(feats):
            message = in_ref[z, f].astype(jnp.float32)
            pairs = [message[:, j * 128 : (j + 1) * 128] for j in range(share // 2)]
            block = jnp.concatenate(pairs, axis=0).astype(out_ref.dtype)
            known.append(message[:, share // 2 * 128 :])
            for c in range(copies):
                out_ref[c, z, f] = block
        facts = [k[i : i + 1] for i in range(2) for k in known]
        facts = jnp.concatenate(facts, axis=0).astype(out_ref.dtype)
        for c in range(copies):
            out_ref[c, z, feats] = facts


def main_kernel(n_pos, n_picks, first, ids_ref, *refs):
    if first:
        x_ref, w_ref, ig_ref, wg_ref = refs
        acc_ref = wg_ref
    else:
        x_ref, w_ref, wg_in_ref, ig_ref, wg_ref, acc_ref = refs
    tiles, feats = x_ref.shape[0], x_ref.shape[1] - 1
    rows = tiles * x_ref.shape[2]
    labels = w_ref.shape[1]
    x = jnp.concatenate([x_ref[:, f].reshape(rows, 128) for f in range(feats)], axis=1)
    w = jnp.concatenate([w_ref[f] for f in range(feats)], axis=1)
    scores = lax.dot_general(w, x, (((1,), (1,)), ((), ())), preferred_element_type=jnp.float32)

    facts = x_ref[:, feats].reshape(rows, 128).astype(jnp.float32).T.astype(jnp.int32)
    base = ids_ref[0] * 2
    pos_slot = facts[:n_pos] - base
    label = facts[n_pos : 2 * n_pos]
    slots = facts[2 * n_pos : 2 * n_pos + 24] - base
    held = (pos_slot == 0) | (pos_slot == 1)
    key = jnp.where(held, pos_slot * (labels // 2) + label, -1)
    word, bit = key >> 5, jnp.left_shift(jnp.int32(1), key & 31)
    lines = lax.broadcasted_iota(jnp.int32, (labels // 32, rows), 0)
    words = jnp.zeros((labels // 32, rows), jnp.int32)
    for p in range(n_pos):
        words = words | jnp.where(word[p : p + 1] == lines, bit[p : p + 1], 0)
    shifts = lax.broadcasted_iota(jnp.int32, (labels // 32, 32, rows), 1)
    bits = lax.shift_right_logical(jnp.broadcast_to(words[:, None, :], shifts.shape), shifts) & 1
    targets = bits.reshape(labels, rows).astype(jnp.float32)
    grad = jax.nn.sigmoid(scores) - targets
    halves = []
    for j in range(2):
        named = jnp.max((slots == j).astype(jnp.float32), axis=0, keepdims=True)
        halves.append(grad[j * (labels // 2) : (j + 1) * (labels // 2)] * named)
    grad = jnp.concatenate(halves, axis=0).astype(jnp.bfloat16)

    ig = lax.dot_general(grad, w, (((0,), (0,)), ((), ())), preferred_element_type=jnp.float32)
    ig = ig.astype(ig_ref.dtype)
    wg = jnp.dot(grad, x, preferred_element_type=jnp.float32)

    step = pl.program_id(0)
    parts = [wg[:, f * 128 : (f + 1) * 128] for f in range(feats)]
    for f in range(feats):
        ig_ref[:, f] = ig[:, f * 128 : (f + 1) * 128].reshape(tiles, -1, 128)

    @pl.when(step == 0)
    def _():
        for f in range(feats):
            acc_ref[f] = parts[f] if first else wg_in_ref[f] + parts[f]

    @pl.when(step > 0)
    def _():
        for f in range(feats):
            acc_ref[f] += parts[f]

    if not first:

        @pl.when(step == pl.num_programs(0) - 1)
        def _():
            wg_ref[...] = acc_ref[...].astype(wg_ref.dtype)


def gradients(ids, x, w, wg, out_type, n_pos, n_picks, steps):
    blocks, width, sub, _ = x.shape
    feats, labels, _ = w.shape
    tiles = blocks // steps
    first = wg is None
    whole = pl.BlockSpec((feats, labels, 128), lambda i, s: (0, 0, 0))
    in_specs = [pl.BlockSpec((tiles, width, sub, 128), lambda i, s: (i, 0, 0, 0)), whole]
    operands = [x, w]
    if not first:
        in_specs.append(whole)
        operands.append(wg)
    flops = 6 * blocks * sub * feats * 128 * labels
    return pl.pallas_call(
        functools.partial(main_kernel, n_pos, n_picks, first),
        out_shape=(
            jax.ShapeDtypeStruct((blocks, feats, sub, 128), out_type),
            jax.ShapeDtypeStruct((feats, labels, 128), jnp.float32 if first else jnp.bfloat16),
        ),
        grid_spec=pltpu.PrefetchScalarGridSpec(
            num_scalar_prefetch=1,
            grid=(steps,),
            in_specs=in_specs,
            out_specs=(pl.BlockSpec((tiles, feats, sub, 128), lambda i, s: (i, 0, 0, 0)), whole),
            scratch_shapes=[] if first else [pltpu.VMEM((feats, labels, 128), jnp.float32)],
        ),
        compiler_params=pltpu.CompilerParams(vmem_limit_bytes=24 * 1024 * 1024),
        cost_estimate=pl.CostEstimate(flops=flops, bytes_accessed=6 << 20, transcendentals=blocks * sub * labels),
    )(ids, *operands)


def collect(parts, axis):
    got = lax.all_to_all(parts.astype(jnp.bfloat16), axis, split_axis=0, concat_axis=0, tiled=True)
    return jnp.sum(got.astype(jnp.float32), axis=0)


def shards(instances, cluster_weights, cluster_home, shortlist, positives):
    ny = lax.axis_size("y")
    rows, part = instances.shape
    owned, labels, _ = cluster_weights.shape
    picks, n_pos = shortlist.shape[1], positives.shape[1]
    clusters = cluster_home.shape[0]
    share = rows // ny
    wide = (share // 2 + 1) * 128
    scale = 1.0 / math.sqrt(rows * picks // owned)
    ids = jnp.stack([lax.axis_index(("x", "z", "c")), lax.axis_index("y")]).astype(jnp.int32)

    w = lax.all_gather(cluster_weights.reshape(owned * labels, part), "y", axis=0)

    smem, vmem = pl.BlockSpec(memory_space=pltpu.SMEM), pl.BlockSpec(memory_space=pltpu.VMEM)
    own = pl.pallas_call(
        prep_kernel,
        out_shape=jax.ShapeDtypeStruct((NZ, ny, 2, wide), jnp.bfloat16),
        in_specs=[smem, smem, vmem, vmem, vmem],
        out_specs=vmem,
        compiler_params=pltpu.CompilerParams(vmem_limit_bytes=52 * 1024 * 1024),
    )(ids, cluster_home, shortlist.T, positives.T, instances)
    line = lax.all_to_all(own.reshape(NZ * ny, 2, wide), ("z", "y"), split_axis=0, concat_axis=0, tiled=True)
    lines = pl.pallas_call(
        repack_kernel,
        out_shape=jax.ShapeDtypeStruct((NX, NZ, ny + 1, share, 128), jnp.bfloat16),
        in_specs=[vmem],
        out_specs=vmem,
        compiler_params=pltpu.CompilerParams(vmem_limit_bytes=8 * 1024 * 1024),
    )(line.reshape(NZ, ny, 2, wide))
    mine = lax.all_to_all(lines, "x", split_axis=0, concat_axis=0, tiled=True).reshape(NX * NZ, ny + 1, share, 128)
    mine, w = lax.optimization_barrier((mine, w))
    swap = [(0, 1), (1, 0)]
    theirs = lax.ppermute(mine, "c", swap)

    ig_mine, wg = gradients(ids, mine, w, None, jnp.float32, n_pos, picks, 2)
    ig_theirs, wg = gradients(ids, theirs, w, wg, jnp.bfloat16, n_pos, picks, 2)
    back = lax.ppermute(ig_theirs, "c", swap)

    weight_sum = lax.psum_scatter(wg, "y", scatter_dimension=0).astype(jnp.float32)
    ig = ig_mine + back.astype(jnp.float32)
    ig = collect(ig.reshape(NX, NZ * ny, share, 128), "x")
    got = lax.all_to_all(ig.astype(jnp.bfloat16), ("z", "y"), split_axis=0, concat_axis=0, tiled=True)
    ig = jnp.sum(got.reshape(NZ, rows, part).astype(jnp.float32), axis=0).astype(jnp.bfloat16)
    weight_grad = (weight_sum * scale).astype(jnp.bfloat16).reshape(owned, labels, part)
    return ig, weight_grad


def solution(mesh):
    fine = Mesh(mesh.devices.reshape(NX, NZ, NC, -1), ("x", "z", "c", "y"))
    dp = ("x", "z", "c")
    return jax.shard_map(
        shards,
        mesh=fine,
        in_specs=(P(dp, "y"), P(dp, None, "y"), P(), P(dp, None), P(dp, None)),
        out_specs=(P(dp, "y"), P(dp, None, "y")),
        check_vma=False,
    )
```

```python
import functools
import math

import jax
import jax.numpy as jnp
from jax import lax
from jax.experimental import pallas as pl
from jax.experimental.pallas import tpu as pltpu
from jax.sharding import Mesh, PartitionSpec as P

NX, NZ, NC = 4, 8, 2
LABEL_BITS = 8


def prep_kernel(ids_ref, home_ref, short_ref, pos_ref, x_ref, out_ref):
    short = short_ref[...]
    pos = pos_ref[...]
    picks, rows = short.shape

    def look(c, slots):
        return jnp.where(short == c, home_ref[c], slots)

    slots = lax.fori_loop(0, home_ref.shape[0], look, jnp.zeros_like(short), unroll=8)
    pick = lax.shift_right_logical(pos, LABEL_BITS)
    pos_slot = jnp.zeros_like(pos)
    for k in range(picks):
        pos_slot = jnp.where(pick == k, slots[k : k + 1, :], pos_slot)
    label = pos & ((1 << LABEL_BITS) - 1)
    pad = jnp.full((128 - picks - 2 * pos.shape[0], rows), -1, jnp.int32)
    facts = jnp.concatenate([pos_slot, label, slots, pad], axis=0).astype(jnp.float32).T
    copies, parts = out_ref.shape[0], out_ref.shape[1]
    share = rows // parts
    x = x_ref[...].astype(jnp.float32)
    line = lax.broadcasted_iota(jnp.int32, (8, 128), 0)
    for t in range(parts):
        known = []
        for i in range(share // 8):
            tile = facts[t * share + i * 8 : t * share + i * 8 + 8]
            known.append(jnp.sum(jnp.where(line == ids_ref[1], tile, 0.0), axis=0, keepdims=True))
        pairs = [x[t * share + j : t * share + j + 2] for j in range(0, share, 2)]
        message = jnp.concatenate([*pairs, jnp.concatenate(known, axis=0)], axis=1).astype(out_ref.dtype)
        for c in range(copies):
            out_ref[c, t] = message


def repack_kernel(in_ref, out_ref):
    copies, zs, _, share, _ = out_ref.shape
    feats = in_ref.shape[1]
    for z in range(zs):
        known = []
        for f in range(feats):
            message = in_ref[z, f].astype(jnp.float32)
            pairs = [message[:, j * 128 : (j + 1) * 128] for j in range(share // 2)]
            block = jnp.concatenate(pairs, axis=0).astype(out_ref.dtype)
            known.append(message[:, share // 2 * 128 :])
            for c in range(copies):
                out_ref[c, z, f] = block
        facts = [k[i : i + 1] for i in range(2) for k in known]
        facts = jnp.concatenate(facts, axis=0).astype(out_ref.dtype)
        for c in range(copies):
            out_ref[c, z, feats] = facts


def main_kernel(n_pos, first, ids_ref, w_hbm, x_ref, *refs):
    if first:
        ig_ref, wg_ref, w_ref, w_sem = refs
    else:
        wg_in_ref, ig_ref, wg_hbm, w_ref, w_sem, wg_ref, wg_sem = refs
    get = pltpu.make_async_copy(w_hbm, w_ref, w_sem)
    get.start()
    tiles, feats = x_ref.shape[0], x_ref.shape[1] - 1
    rows = tiles * x_ref.shape[2]
    labels = w_ref.shape[1]

    facts = x_ref[:, feats].reshape(rows, 128).astype(jnp.float32).T.astype(jnp.int32)
    base = ids_ref[0] * 2
    pos_slot = facts[:n_pos] - base
    label = facts[n_pos : 2 * n_pos]
    slots = facts[2 * n_pos : 2 * n_pos + 24] - base
    held = (pos_slot == 0) | (pos_slot == 1)
    key = jnp.where(held, pos_slot * (labels // 2) + label, -1)
    word, bit = key >> 5, jnp.left_shift(jnp.int32(1), key & 31)
    lines = lax.broadcasted_iota(jnp.int32, (labels // 32, rows), 0)
    words = jnp.zeros((labels // 32, rows), jnp.int32)
    for p in range(n_pos):
        words = words | jnp.where(word[p : p + 1] == lines, bit[p : p + 1], 0)
    x = jnp.concatenate([x_ref[:, f].reshape(rows, 128) for f in range(feats)], axis=1)

    get.wait()
    w = jnp.concatenate([w_ref[f] for f in range(feats)], axis=1)
    scores = lax.dot_general(w, x, (((1,), (1,)), ((), ())), preferred_element_type=jnp.float32)
    shifts = lax.broadcasted_iota(jnp.int32, (labels // 32, 32, rows), 1)
    bits = lax.shift_right_logical(jnp.broadcast_to(words[:, None, :], shifts.shape), shifts) & 1
    targets = bits.reshape(labels, rows).astype(jnp.float32)
    grad = jax.nn.sigmoid(scores) - targets
    halves = []
    for j in range(2):
        named = jnp.max((slots == j).astype(jnp.float32), axis=0, keepdims=True)
        halves.append(grad[j * (labels // 2) : (j + 1) * (labels // 2)] * named)
    grad = jnp.concatenate(halves, axis=0).astype(jnp.bfloat16)

    puts = []
    for f in range(0, feats, 2):
        wg = jnp.dot(grad, x[:, f * 128 : (f + 2) * 128], preferred_element_type=jnp.float32)
        for i in range(2):
            part = wg[:, i * 128 : (i + 1) * 128]
            wg_ref[f + i] = part if first else wg_in_ref[f + i] + part
        if not first:
            puts.append(pltpu.make_async_copy(wg_ref.at[pl.ds(f, 2)], wg_hbm.at[pl.ds(f, 2)], wg_sem.at[f // 2]))
            puts[-1].start()
    ig = lax.dot_general(grad, w, (((0,), (0,)), ((), ())), preferred_element_type=jnp.float32)
    ig = ig.astype(ig_ref.dtype)
    for f in range(feats):
        ig_ref[:, f] = ig[:, f * 128 : (f + 1) * 128].reshape(tiles, -1, 128)
    for put in puts:
        put.wait()


def gradients(ids, x, w, wg, out_type, n_pos):
    blocks, width, sub, _ = x.shape
    feats, labels, _ = w.shape
    first = wg is None
    smem, vmem = pl.BlockSpec(memory_space=pltpu.SMEM), pl.BlockSpec(memory_space=pltpu.VMEM)
    hbm = pl.BlockSpec(memory_space=pltpu.HBM)
    scratch = [pltpu.VMEM((feats, labels, 128), jnp.bfloat16), pltpu.SemaphoreType.DMA]
    if not first:
        scratch += [pltpu.VMEM((feats, labels, 128), jnp.float32), pltpu.SemaphoreType.DMA((feats // 2,))]
    return pl.pallas_call(
        functools.partial(main_kernel, n_pos, first),
        out_shape=(
            jax.ShapeDtypeStruct((blocks, feats, sub, 128), out_type),
            jax.ShapeDtypeStruct((feats, labels, 128), jnp.float32),
        ),
        in_specs=[smem, hbm, vmem] + [vmem] * (not first),
        out_specs=(vmem, vmem if first else hbm),
        scratch_shapes=scratch,
        compiler_params=pltpu.CompilerParams(vmem_limit_bytes=28 * 1024 * 1024),
        cost_estimate=pl.CostEstimate(
            flops=6 * blocks * sub * feats * 128 * labels, bytes_accessed=6 << 20, transcendentals=blocks * sub * labels
        ),
    )(ids, w, x, *([] if first else [wg]))


def collect(parts, axis):
    got = lax.all_to_all(parts.astype(jnp.bfloat16), axis, split_axis=0, concat_axis=0, tiled=True)
    return jnp.sum(got.astype(jnp.float32), axis=0)


def shards(instances, cluster_weights, cluster_home, shortlist, positives):
    ny = lax.axis_size("y")
    rows, part = instances.shape
    owned, labels, _ = cluster_weights.shape
    picks, n_pos = shortlist.shape[1], positives.shape[1]
    share = rows // ny
    wide = (share // 2 + 1) * 128
    scale = 1.0 / math.sqrt(rows * picks // owned)
    ids = jnp.stack([lax.axis_index(("x", "z", "c")), lax.axis_index("y")]).astype(jnp.int32)

    w = lax.all_gather(cluster_weights.reshape(owned * labels, part), "y", axis=0)

    smem, vmem = pl.BlockSpec(memory_space=pltpu.SMEM), pl.BlockSpec(memory_space=pltpu.VMEM)
    own = pl.pallas_call(
        prep_kernel,
        out_shape=jax.ShapeDtypeStruct((NZ, ny, 2, wide), jnp.bfloat16),
        in_specs=[smem, smem, vmem, vmem, vmem],
        out_specs=vmem,
    )(ids, cluster_home, shortlist.T, positives.T, instances)
    line = lax.all_to_all(own.reshape(NZ * ny, 2, wide), ("z", "y"), split_axis=0, concat_axis=0, tiled=True)
    lines = pl.pallas_call(
        repack_kernel,
        out_shape=jax.ShapeDtypeStruct((NX, NZ, ny + 1, share, 128), jnp.bfloat16),
        in_specs=[vmem],
        out_specs=vmem,
        compiler_params=pltpu.CompilerParams(vmem_limit_bytes=8 * 1024 * 1024),
    )(line.reshape(NZ, ny, 2, wide))
    mine = lax.all_to_all(lines, "x", split_axis=0, concat_axis=0, tiled=True).reshape(NX * NZ, ny + 1, share, 128)
    mine, w = lax.optimization_barrier((mine, w))
    swap = [(0, 1), (1, 0)]
    theirs = lax.ppermute(mine, "c", swap)

    ig_mine, wg = gradients(ids, mine, w, None, jnp.float32, n_pos)
    ig_theirs, wg = gradients(ids, theirs, w, wg, jnp.bfloat16, n_pos)
    back = lax.ppermute(ig_theirs, "c", swap)

    weight_sum = lax.psum_scatter(wg, "y", scatter_dimension=0)
    ig = ig_mine + back.astype(jnp.float32)
    ig = collect(ig.reshape(NX, NZ * ny, share, 128), "x")
    got = lax.all_to_all(ig.astype(jnp.bfloat16), ("z", "y"), split_axis=0, concat_axis=0, tiled=True)
    ig = jnp.sum(got.reshape(NZ, rows, part).astype(jnp.float32), axis=0).astype(jnp.bfloat16)
    weight_grad = (weight_sum * scale).astype(jnp.bfloat16).reshape(owned, labels, part)
    return ig, weight_grad


def solution(mesh):
    fine = Mesh(mesh.devices.reshape(NX, NZ, NC, -1), ("x", "z", "c", "y"))
    dp = ("x", "z", "c")
    return jax.shard_map(
        shards,
        mesh=fine,
        in_specs=(P(dp, "y"), P(dp, None, "y"), P(), P(dp, None), P(dp, None)),
        out_specs=(P(dp, "y"), P(dp, None, "y")),
        check_vma=False,
    )
```

```python
import functools
import math

import jax
import jax.numpy as jnp
from jax import lax
from jax.experimental import pallas as pl
from jax.experimental.pallas import tpu as pltpu
from jax.sharding import Mesh, PartitionSpec as P

NX, NZ, NC = 4, 8, 2
LABEL_BITS = 8


def prep_kernel(place_ref, home_ref, short_ref, pos_ref, out_ref, full_ref):
    short = short_ref[...]
    pos = pos_ref[...]
    picks, rows = short.shape

    def look(c, slots):
        return jnp.where(short == c, home_ref[c], slots)

    slots = lax.fori_loop(0, home_ref.shape[0], look, jnp.zeros_like(short), unroll=8)
    pick = lax.shift_right_logical(pos, LABEL_BITS)
    pos_slot = jnp.zeros_like(pos)
    for k in range(picks):
        pos_slot = jnp.where(pick == k, slots[k : k + 1, :], pos_slot)
    label = pos & ((1 << LABEL_BITS) - 1)
    pad = jnp.full((128 - picks - 2 * pos.shape[0], rows), -1, jnp.int32)
    facts = jnp.concatenate([pos_slot, label, slots, pad], axis=0).astype(jnp.float32).T
    full_ref[...] = facts
    share = out_ref.shape[0]
    first = pl.multiple_of(place_ref[0] * share, share)
    out_ref[...] = full_ref[pl.ds(first, share), :].astype(out_ref.dtype)


def copy_kernel(*refs):
    *in_refs, out_ref = refs
    for c in range(out_ref.shape[0]):
        at = 0
        for ref in in_refs:
            out_ref[c, at : at + ref.shape[0]] = ref[...]
            at += ref.shape[0]


def copies(number, *blocks):
    rest = blocks[0].shape[1:]
    vmem = pl.BlockSpec(memory_space=pltpu.VMEM)
    return pl.pallas_call(
        copy_kernel,
        out_shape=jax.ShapeDtypeStruct((number, sum(b.shape[0] for b in blocks), *rest), blocks[0].dtype),
        in_specs=[vmem] * len(blocks),
        out_specs=vmem,
        compiler_params=pltpu.CompilerParams(vmem_limit_bytes=8 * 1024 * 1024),
    )(*blocks)


def main_kernel(n_pos, first, me_ref, w_hbm, x_ref, *refs):
    if first:
        ig_ref, wg_ref, w_ref, w_sem = refs
    else:
        wg_in_ref, ig_ref, wg_hbm, w_ref, w_sem, wg_ref, wg_sem = refs
    get = pltpu.make_async_copy(w_hbm, w_ref, w_sem)
    get.start()
    tiles, feats = x_ref.shape[0], x_ref.shape[1] - 1
    rows = tiles * x_ref.shape[2]
    labels = w_ref.shape[1]

    facts = x_ref[:, feats].reshape(rows, 128).astype(jnp.float32).T.astype(jnp.int32)
    base = me_ref[0] * 2
    pos_slot = facts[:n_pos] - base
    label = facts[n_pos : 2 * n_pos]
    slots = facts[2 * n_pos : 2 * n_pos + 24] - base
    held = (pos_slot == 0) | (pos_slot == 1)
    key = jnp.where(held, pos_slot * (labels // 2) + label, -1)
    word, bit = key >> 5, jnp.left_shift(jnp.int32(1), key & 31)
    lines = lax.broadcasted_iota(jnp.int32, (labels // 32, rows), 0)
    words = jnp.zeros((labels // 32, rows), jnp.int32)
    for p in range(n_pos):
        words = words | jnp.where(word[p : p + 1] == lines, bit[p : p + 1], 0)
    x = jnp.concatenate([x_ref[:, f].reshape(rows, 128) for f in range(feats)], axis=1)

    get.wait()
    w = jnp.concatenate([w_ref[f] for f in range(feats)], axis=1)
    scores = lax.dot_general(w, x, (((1,), (1,)), ((), ())), preferred_element_type=jnp.float32)
    shifts = lax.broadcasted_iota(jnp.int32, (labels // 32, 32, rows), 1)
    bits = lax.shift_right_logical(jnp.broadcast_to(words[:, None, :], shifts.shape), shifts) & 1
    targets = bits.reshape(labels, rows).astype(jnp.float32)
    grad = jax.nn.sigmoid(scores) - targets
    halves = []
    for j in range(2):
        named = jnp.max((slots == j).astype(jnp.float32), axis=0, keepdims=True)
        halves.append(grad[j * (labels // 2) : (j + 1) * (labels // 2)] * named)
    grad = jnp.concatenate(halves, axis=0).astype(jnp.bfloat16)

    puts = []
    for f in range(0, feats, 2):
        wg = jnp.dot(grad, x[:, f * 128 : (f + 2) * 128], preferred_element_type=jnp.float32)
        for i in range(2):
            part = wg[:, i * 128 : (i + 1) * 128]
            wg_ref[f + i] = part if first else wg_in_ref[f + i] + part
        if not first:
            puts.append(pltpu.make_async_copy(wg_ref.at[pl.ds(f, 2)], wg_hbm.at[pl.ds(f, 2)], wg_sem.at[f // 2]))
            puts[-1].start()
    ig = lax.dot_general(grad, w, (((0,), (0,)), ((), ())), preferred_element_type=jnp.float32)
    ig = ig.astype(ig_ref.dtype)
    for f in range(feats):
        ig_ref[:, f] = ig[:, f * 128 : (f + 1) * 128].reshape(tiles, -1, 128)
    for put in puts:
        put.wait()


def gradients(me, x, w, wg, out_type, n_pos):
    blocks, width, sub, _ = x.shape
    feats, labels, _ = w.shape
    first = wg is None
    smem, vmem = pl.BlockSpec(memory_space=pltpu.SMEM), pl.BlockSpec(memory_space=pltpu.VMEM)
    hbm = pl.BlockSpec(memory_space=pltpu.HBM)
    scratch = [pltpu.VMEM((feats, labels, 128), jnp.bfloat16), pltpu.SemaphoreType.DMA]
    if not first:
        scratch += [pltpu.VMEM((feats, labels, 128), jnp.float32), pltpu.SemaphoreType.DMA((feats // 2,))]
    return pl.pallas_call(
        functools.partial(main_kernel, n_pos, first),
        out_shape=(
            jax.ShapeDtypeStruct((blocks, feats, sub, 128), out_type),
            jax.ShapeDtypeStruct((feats, labels, 128), jnp.float32),
        ),
        in_specs=[smem, hbm, vmem] + [vmem] * (not first),
        out_specs=(vmem, vmem if first else hbm),
        scratch_shapes=scratch,
        compiler_params=pltpu.CompilerParams(vmem_limit_bytes=28 * 1024 * 1024),
        cost_estimate=pl.CostEstimate(
            flops=6 * blocks * sub * feats * 128 * labels, bytes_accessed=6 << 20, transcendentals=blocks * sub * labels
        ),
    )(me, w, x, *([] if first else [wg]))


def collect(parts, axis):
    got = lax.all_to_all(parts.astype(jnp.bfloat16), axis, split_axis=0, concat_axis=0, tiled=True)
    return jnp.sum(got.astype(jnp.float32), axis=0)


def shards(instances, cluster_weights, cluster_home, shortlist, positives):
    ny = lax.axis_size("y")
    rows, part = instances.shape
    owned, labels, _ = cluster_weights.shape
    picks, n_pos = shortlist.shape[1], positives.shape[1]
    share = rows // ny
    scale = 1.0 / math.sqrt(rows * picks // owned)
    me, place = lax.axis_index(("x", "z", "c")).reshape(1), lax.axis_index("y").reshape(1)

    w = lax.all_gather(cluster_weights.reshape(owned * labels, part), "y", axis=0)

    smem, vmem = pl.BlockSpec(memory_space=pltpu.SMEM), pl.BlockSpec(memory_space=pltpu.VMEM)
    own = lax.all_to_all(instances.reshape(ny, share, part), "y", split_axis=0, concat_axis=0, tiled=True)
    facts = pl.pallas_call(
        prep_kernel,
        out_shape=jax.ShapeDtypeStruct((share, 128), jnp.bfloat16),
        in_specs=[smem, smem, vmem, vmem],
        out_specs=vmem,
        scratch_shapes=[pltpu.VMEM((rows, 128), jnp.float32)],
    )(place, cluster_home, shortlist.T, positives.T)
    line = lax.all_to_all(copies(NZ, own, facts[None]), "z", split_axis=0, concat_axis=0, tiled=True)
    lines = copies(NX, line)
    mine = lax.all_to_all(lines, "x", split_axis=0, concat_axis=0, tiled=True).reshape(NX * NZ, ny + 1, share, 128)
    mine, w = lax.optimization_barrier((mine, w))
    swap = [(0, 1), (1, 0)]
    theirs = lax.ppermute(mine, "c", swap)

    ig_mine, wg = gradients(me, mine, w, None, jnp.float32, n_pos)
    ig_theirs, wg = gradients(me, theirs, w, wg, jnp.bfloat16, n_pos)
    back = lax.ppermute(ig_theirs, "c", swap)

    weight_sum = lax.psum_scatter(wg, "y", scatter_dimension=0)
    ig = ig_mine + back.astype(jnp.float32)
    ig = collect(ig.reshape(NX, NZ * ny, share, 128), "x")
    got = lax.all_to_all(ig.astype(jnp.bfloat16), ("z", "y"), split_axis=0, concat_axis=0, tiled=True)
    ig = jnp.sum(got.reshape(NZ, rows, part).astype(jnp.float32), axis=0).astype(jnp.bfloat16)
    weight_grad = (weight_sum * scale).astype(jnp.bfloat16).reshape(owned, labels, part)
    return ig, weight_grad


def solution(mesh):
    fine = Mesh(mesh.devices.reshape(NX, NZ, NC, -1), ("x", "z", "c", "y"))
    dp = ("x", "z", "c")
    return jax.shard_map(
        shards,
        mesh=fine,
        in_specs=(P(dp, "y"), P(dp, None, "y"), P(), P(dp, None), P(dp, None)),
        out_specs=(P(dp, "y"), P(dp, None, "y")),
        check_vma=False,
    )
```

```python
import functools
import math

import jax
import jax.numpy as jnp
from jax import lax
from jax.experimental import pallas as pl
from jax.experimental.pallas import tpu as pltpu
from jax.sharding import Mesh, PartitionSpec as P

NX, NZ, NC = 4, 8, 2
LABEL_BITS = 8


def prep_kernel(place_ref, home_ref, short_ref, pos_ref, out_ref, full_ref):
    short = short_ref[...]
    pos = pos_ref[...]
    picks, rows = short.shape

    def look(c, slots):
        return jnp.where(short == c, home_ref[c], slots)

    slots = lax.fori_loop(0, home_ref.shape[0], look, jnp.zeros_like(short), unroll=8)
    pick = lax.shift_right_logical(pos, LABEL_BITS)
    pos_slot = jnp.zeros_like(pos)
    for k in range(picks):
        pos_slot = jnp.where(pick == k, slots[k : k + 1, :], pos_slot)
    label = pos & ((1 << LABEL_BITS) - 1)
    pad = jnp.full((128 - picks - 2 * pos.shape[0], rows), -1, jnp.int32)
    facts = jnp.concatenate([pos_slot, label, slots, pad], axis=0).astype(jnp.float32).T
    full_ref[...] = facts
    share = out_ref.shape[0]
    first = pl.multiple_of(place_ref[0] * share, share)
    out_ref[...] = full_ref[pl.ds(first, share), :].astype(out_ref.dtype)


def copy_kernel(*refs):
    *in_refs, out_ref = refs
    for c in range(out_ref.shape[0]):
        at = 0
        for ref in in_refs:
            out_ref[c, at : at + ref.shape[0]] = ref[...]
            at += ref.shape[0]


def copies(number, *blocks):
    rest = blocks[0].shape[1:]
    vmem = pl.BlockSpec(memory_space=pltpu.VMEM)
    return pl.pallas_call(
        copy_kernel,
        out_shape=jax.ShapeDtypeStruct((number, sum(b.shape[0] for b in blocks), *rest), blocks[0].dtype),
        in_specs=[vmem] * len(blocks),
        out_specs=vmem,
        compiler_params=pltpu.CompilerParams(vmem_limit_bytes=8 * 1024 * 1024),
    )(*blocks)


def main_kernel(n_pos, first, me_ref, w_hbm, x_in, *refs):
    if first:
        ig_ref, wg_ref, w_ref, w_sem = refs
        x_ref = x_in
    else:
        wg_in_ref, ig_ref, wg_hbm, w_ref, w_sem, wg_ref, wg_sem, x_ref, x_sem = refs
    get = pltpu.make_async_copy(w_hbm, w_ref, w_sem)
    tiles, feats = x_ref.shape[0], x_ref.shape[1] - 1
    if not first:
        get_facts = pltpu.make_async_copy(x_in.at[:, pl.ds(feats, 1)], x_ref.at[:, pl.ds(feats, 1)], x_sem.at[0])
        get_rows = pltpu.make_async_copy(x_in.at[:, pl.ds(0, feats)], x_ref.at[:, pl.ds(0, feats)], x_sem.at[1])
        get_facts.start()
        get_rows.start()
    get.start()
    if not first:
        get_facts.wait()
    rows = tiles * x_ref.shape[2]
    labels = w_ref.shape[1]

    facts = x_ref[:, feats].reshape(rows, 128).astype(jnp.float32).T.astype(jnp.int32)
    base = me_ref[0] * 2
    pos_slot = facts[:n_pos] - base
    label = facts[n_pos : 2 * n_pos]
    slots = facts[2 * n_pos : 2 * n_pos + 24] - base
    held = (pos_slot == 0) | (pos_slot == 1)
    key = jnp.where(held, pos_slot * (labels // 2) + label, -1)
    word, bit = key >> 5, jnp.left_shift(jnp.int32(1), key & 31)
    lines = lax.broadcasted_iota(jnp.int32, (labels // 32, rows), 0)
    words = jnp.zeros((labels // 32, rows), jnp.int32)
    for p in range(n_pos):
        words = words | jnp.where(word[p : p + 1] == lines, bit[p : p + 1], 0)
    if not first:
        get_rows.wait()
    x = jnp.concatenate([x_ref[:, f].reshape(rows, 128) for f in range(feats)], axis=1)

    get.wait()
    w = jnp.concatenate([w_ref[f] for f in range(feats)], axis=1)
    scores = lax.dot_general(w, x, (((1,), (1,)), ((), ())), preferred_element_type=jnp.float32)
    shifts = lax.broadcasted_iota(jnp.int32, (labels // 32, 32, rows), 1)
    bits = lax.shift_right_logical(jnp.broadcast_to(words[:, None, :], shifts.shape), shifts) & 1
    targets = bits.reshape(labels, rows).astype(jnp.float32)
    grad = jax.nn.sigmoid(scores) - targets
    halves = []
    for j in range(2):
        named = jnp.max((slots == j).astype(jnp.float32), axis=0, keepdims=True)
        halves.append(grad[j * (labels // 2) : (j + 1) * (labels // 2)] * named)
    grad = jnp.concatenate(halves, axis=0).astype(jnp.bfloat16)

    puts = []
    for f in range(0, feats, 2):
        wg = jnp.dot(grad, x[:, f * 128 : (f + 2) * 128], preferred_element_type=jnp.float32)
        for i in range(2):
            part = wg[:, i * 128 : (i + 1) * 128]
            wg_ref[f + i] = part if first else wg_in_ref[f + i] + part
        if not first:
            puts.append(pltpu.make_async_copy(wg_ref.at[pl.ds(f, 2)], wg_hbm.at[pl.ds(f, 2)], wg_sem.at[f // 2]))
            puts[-1].start()
    ig = lax.dot_general(grad, w, (((0,), (0,)), ((), ())), preferred_element_type=jnp.float32)
    ig = ig.astype(ig_ref.dtype)
    for f in range(feats):
        ig_ref[:, f] = ig[:, f * 128 : (f + 1) * 128].reshape(tiles, -1, 128)
    for put in puts:
        put.wait()


def gradients(me, x, w, wg, out_type, n_pos):
    blocks, width, sub, _ = x.shape
    feats, labels, _ = w.shape
    first = wg is None
    smem, vmem = pl.BlockSpec(memory_space=pltpu.SMEM), pl.BlockSpec(memory_space=pltpu.VMEM)
    hbm = pl.BlockSpec(memory_space=pltpu.HBM)
    scratch = [pltpu.VMEM((feats, labels, 128), jnp.bfloat16), pltpu.SemaphoreType.DMA]
    if not first:
        scratch += [pltpu.VMEM((feats, labels, 128), jnp.float32), pltpu.SemaphoreType.DMA((feats // 2,))]
        scratch += [pltpu.VMEM(x.shape, jnp.bfloat16), pltpu.SemaphoreType.DMA((2,))]
    return pl.pallas_call(
        functools.partial(main_kernel, n_pos, first),
        out_shape=(
            jax.ShapeDtypeStruct((blocks, feats, sub, 128), out_type),
            jax.ShapeDtypeStruct((feats, labels, 128), jnp.float32),
        ),
        in_specs=[smem, hbm, vmem] if first else [smem, hbm, hbm, vmem],
        out_specs=(vmem, vmem if first else hbm),
        scratch_shapes=scratch,
        compiler_params=pltpu.CompilerParams(vmem_limit_bytes=28 * 1024 * 1024),
        cost_estimate=pl.CostEstimate(
            flops=6 * blocks * sub * feats * 128 * labels, bytes_accessed=6 << 20, transcendentals=blocks * sub * labels
        ),
    )(me, w, x, *([] if first else [wg]))


def collect(parts, axis):
    got = lax.all_to_all(parts.astype(jnp.bfloat16), axis, split_axis=0, concat_axis=0, tiled=True)
    return jnp.sum(got.astype(jnp.float32), axis=0)


def shards(instances, cluster_weights, cluster_home, shortlist, positives):
    ny = lax.axis_size("y")
    rows, part = instances.shape
    owned, labels, _ = cluster_weights.shape
    picks, n_pos = shortlist.shape[1], positives.shape[1]
    share = rows // ny
    scale = 1.0 / math.sqrt(rows * picks // owned)
    me, place = lax.axis_index(("x", "z", "c")).reshape(1), lax.axis_index("y").reshape(1)

    w = lax.all_gather(cluster_weights.reshape(owned * labels, part), "y", axis=0)

    smem, vmem = pl.BlockSpec(memory_space=pltpu.SMEM), pl.BlockSpec(memory_space=pltpu.VMEM)
    own = lax.all_to_all(instances.reshape(ny, share, part), "y", split_axis=0, concat_axis=0, tiled=True)
    facts = pl.pallas_call(
        prep_kernel,
        out_shape=jax.ShapeDtypeStruct((share, 128), jnp.bfloat16),
        in_specs=[smem, smem, vmem, vmem],
        out_specs=vmem,
        scratch_shapes=[pltpu.VMEM((rows, 128), jnp.float32)],
    )(place, cluster_home, shortlist.T, positives.T)
    line = lax.all_to_all(copies(NZ, own, facts[None]), "z", split_axis=0, concat_axis=0, tiled=True)
    lines = copies(NX, line)
    mine = lax.all_to_all(lines, "x", split_axis=0, concat_axis=0, tiled=True).reshape(NX * NZ, ny + 1, share, 128)
    mine, w = lax.optimization_barrier((mine, w))
    swap = [(0, 1), (1, 0)]
    theirs = lax.ppermute(mine, "c", swap)

    ig_mine, wg = gradients(me, mine, w, None, jnp.float32, n_pos)
    ig_theirs, wg = gradients(me, theirs, w, wg, jnp.bfloat16, n_pos)
    back = lax.ppermute(ig_theirs, "c", swap)

    weight_sum = lax.psum_scatter(wg, "y", scatter_dimension=0)
    ig = ig_mine + back.astype(jnp.float32)
    ig = collect(ig.reshape(NX, NZ * ny, share, 128), "x")
    got = lax.all_to_all(ig.astype(jnp.bfloat16), ("z", "y"), split_axis=0, concat_axis=0, tiled=True)
    ig = jnp.sum(got.reshape(NZ, rows, part).astype(jnp.float32), axis=0).astype(jnp.bfloat16)
    weight_grad = (weight_sum * scale).astype(jnp.bfloat16).reshape(owned, labels, part)
    return ig, weight_grad


def solution(mesh):
    fine = Mesh(mesh.devices.reshape(NX, NZ, NC, -1), ("x", "z", "c", "y"))
    dp = ("x", "z", "c")
    return jax.shard_map(
        shards,
        mesh=fine,
        in_specs=(P(dp, "y"), P(dp, None, "y"), P(), P(dp, None), P(dp, None)),
        out_specs=(P(dp, "y"), P(dp, None, "y")),
        check_vma=False,
    )
```
